32 devices in a mesh: parts: 2 (over y), leaf: 4 (over z), col: 2 (over x), rep: 2 (over core).
Axes of the slice: x: 2, y: 2, z: 4, core: 2. Of those that a mesh axis runs over, the one named last changes fastest.
Arguments:
- leaf_inverse: bfloat16 [8, 2048, 2048], P(('parts', 'leaf')), parts along dimension 0, may hold values from -0.125 to 0.125
- leaf_coupling: bfloat16 [8, 2, 128, 2048], P(('parts', 'leaf')), parts along dimension 0, may hold values from -0.0625 to 0.0625
- leaf_rows: int32 [8, 2, 128], P(('parts', 'leaf')), parts along dimension 0, may hold values from 0 to 255, as said below
- leaf_size: int32 [8], P(('parts', 'leaf')), parts along dimension 0, may hold values from 1024 to 2048, as said below
- sep_inverse: bfloat16 [8, 256, 256], P(('parts', 'leaf')), parts along dimension 0, may hold values from -0.375 to 0.375
- sep_coupling: bfloat16 [8, 1, 256, 256], P(('parts', 'leaf')), parts along dimension 0, may hold values from -0.1875 to 0.1875
- rhs_leaf: bfloat16 [16384, 512], P(('parts', 'leaf'), 'col'), parts along dimension 0, may hold values from -6 to 6
- rhs_sep: bfloat16 [2048, 512], P(('parts', 'leaf'), 'col'), parts along dimension 0, may hold values from -6 to 6
- sensor_owner: int32 [4096, 1], P(('parts', 'leaf', 'rep')), parts along dimension 0, may hold values from 0 to 3; in each aligned block of 256 rows (0 to 255, 256 to 511, ...) at most 128 rows name the same one
- sensor_row: int32 [4096], P(('parts', 'leaf', 'rep')), parts along dimension 0, may hold values from 0 to 1023
- sensor_weight: float32 [4096], P(('parts', 'leaf', 'rep')), parts along dimension 0, may hold values from 0.1 to 10
Outputs:
- x_leaf: bfloat16 [16384, 512], P(('parts', 'leaf'), 'col'), parts along dimension 0
- x_sep: bfloat16 [2048, 512], P(('parts', 'leaf'), 'col'), parts along dimension 0
- gram: float32 [1024, 512], P(('parts', 'leaf', 'rep'), 'col'), parts along dimension 0
The draws below stay inside these ranges and needn't reach their ends.
There are 2 independent parts, one for each index of `parts`. The reference program is written for one: setup_inputs(seed, part) draws one part's arguments, and reference() takes and returns one part's arrays. A program takes and returns all parts, laid end to end along the dimension named above; each array names one. Nothing has to cross between parts.
Inputs may be any that keep to these rules, and one draw needn't show every extreme that they name: `leaf_rows`: the 128 row indices of one leaf and level are distinct. `leaf_size`: at least one leaf supernode is full. `sensor_owner`: among the sensors of one device, at most 128 lie in one leaf.
All inputs are finite; a program needn't handle non-finite values.
Results may differ from the reference program's by a relative error of at most 0.0059.
Values may be sent and summed in bfloat16 or wider, within the bound.
A program may use at most 64 MiB of HBM per device.

```python
import math
import jax
import jax.numpy as jnp
import numpy as np

LS = 2048
SS = 256
KR = 128
NCOL = 512
SENS_DEV = 256
LEVELS = 2
CAP = 128
NSENS = 2048
N_LEAF = 4


def draw_leaf_size(key, part):
    first_key, second_key = jax.random.split(jax.random.fold_in(key, 11))
    drawn = jax.random.randint(first_key, (N_LEAF,), LS // 2, LS + 1)
    full_place = jax.random.randint(second_key, (), 0, N_LEAF)
    return drawn.at[full_place].set(LS).astype(jnp.int32)


def pick_rows(single_key):
    return jax.random.permutation(single_key, SS)[:KR]


def draw_leaf_rows(key, part):
    many_keys = jax.random.split(jax.random.fold_in(key, 23), N_LEAF * LEVELS)
    picked = jax.vmap(pick_rows)(many_keys)
    return picked.reshape(N_LEAF, LEVELS, KR).astype(jnp.int32)


def place_ends(array, rng, smallest, largest):
    spot = [jax.random.randint(jax.random.fold_in(rng, axis), (), 0, length) for axis, length in enumerate(array.shape)]
    widest = array.shape.index(max(array.shape))
    beside = spot[:widest] + [(spot[widest] + 1) % array.shape[widest]] + spot[widest + 1:]
    return array.at[tuple(spot)].set(smallest).at[tuple(beside)].set(largest)


def shard_levels(rng, shape, shards, low, largest):
    level = 1.0
    for dim, parts in shards:
        heights = jax.random.uniform(jax.random.fold_in(jax.random.fold_in(rng, 6), dim), (parts,), jnp.float32, low / len(shards), largest / len(shards))
        level = level * jnp.repeat(jnp.exp(heights), shape[dim] // parts).reshape((-1,) + (1,) * (len(shape) - 1 - dim))
    return level


def deal_out(own_key, own, number, rows, number_of, top, most, lean):
    ranking = jax.random.permutation(own_key, number_of)
    heavy_load, ordinary = shares(number_of, rows * top, most, lean, True), shares(number_of, rows * top, most, lean, False)
    places = jnp.arange(number_of)

    def named(sizes, offset_by):
        used = int((sizes > 0).sum())
        fixed = max(1, used // 4)
        moved = fixed + (places - fixed + offset_by * (used - fixed)) % max(1, number_of - fixed)
        return jnp.zeros((number_of,), jnp.int32).at[ranking[jnp.where(places < fixed, places, moved)]].set(jnp.asarray(sizes, jnp.int32))

    sizes = jnp.where(number % 4 == 0, named(heavy_load, number // 4), named(ordinary, number - number // 4 - 1))
    mixed = jax.random.permutation(jax.random.fold_in(own, 3), number_of)
    source_of, sink = mixed[0:number_of // 2 * 2:2], mixed[1:number_of // 2 * 2:2]
    room = jnp.minimum(sizes[source_of] - 1, most - sizes[sink]) // 2
    room = jnp.where((source_of == ranking[0]) | (sink == ranking[0]) | (sizes[sink] == 0), 0, jnp.maximum(room, 0))
    moved = jax.random.randint(jax.random.fold_in(own, 4), (number_of // 2,), 0, 1 << 20) % (room + 1)
    sizes = sizes.at[source_of].add(-moved).at[sink].add(moved)
    items = jnp.searchsorted(jnp.cumsum(sizes), jnp.arange(rows * top), side="right").astype(jnp.int32)
    table = items.reshape(top, rows).T
    table = table[jax.random.permutation(jax.random.fold_in(own, 1), rows)]
    offset_by = jax.random.randint(jax.random.fold_in(own, 2), (rows, 1), 0, top)
    return jnp.take_along_axis(table, (jnp.arange(top)[None, :] + offset_by) % top, axis=1)


def shares(count, total, limit, skew, full):
    loads = [(1 << 20) // math.isqrt(grade ** skew) + 1 for grade in range(1, count + 1)]
    largest = limit if full else min(limit, max(-(-total // count), total * loads[0] // sum(loads)))
    least = 1 if total - largest >= count - 1 else 0
    counts, rest = [largest] + [least] * (count - 1), total - largest - least * (count - 1)
    while rest > 0:
        movable = [i for i in range(1, count) if counts[i] < largest] or [i for i in range(1, count) if counts[i] < limit]
        whole, remaining = sum([loads[i] for i in movable]), rest
        for i in movable:
            extra = min(limit - counts[i], max(1, remaining * loads[i] // whole), rest)
            counts[i] = counts[i] + extra
            rest = rest - extra
    return np.array(counts)


def centred(own_key, shape, deviation, bound, cuts=(), dtype=jnp.bfloat16):
    entries = jax.random.normal(own_key, shape, jnp.float32) * deviation
    if len(cuts) > 0:
        entries = shard_levels(own_key, shape, cuts, -0.22, 0.18) * entries
    return jnp.clip(entries, min=-bound, max=bound).astype(dtype)


def setup_inputs(seed: int = 0, part: int = 0) -> dict:
    keys = jax.random.split(jax.random.key(seed), 12)
    own_keys = jax.random.split(jax.random.fold_in(keys[11], part), 12)
    leaf_inverse = centred(own_keys[0], (N_LEAF, LS, LS), LS ** -0.5, 0.125, ((0, 4),))
    leaf_coupling = centred(own_keys[1], (N_LEAF, LEVELS, KR, LS), (4 * LS) ** -0.5, 0.0625, ((0, 4),))
    leaf_rows = draw_leaf_rows(jax.random.fold_in(jax.random.fold_in(keys[11], part), 71), part)
    leaf_size = draw_leaf_size(jax.random.fold_in(jax.random.fold_in(keys[11], part), 71), part)
    sep_inverse = centred(own_keys[4], (N_LEAF, SS, SS), SS ** -0.5, 0.375, ((0, 4),))
    sep_coupling = centred(own_keys[5], (N_LEAF, LEVELS - 1, SS, SS), (4 * SS) ** -0.5, 0.1875, ((0, 4),))
    rhs_leaf = centred(own_keys[6], (N_LEAF * LS, NCOL), 1.0, 6.0, ((0, 4), (1, 2)))
    rhs_sep = centred(own_keys[7], (N_LEAF * SS, NCOL), 1.0, 6.0, ((0, 4), (1, 2)))
    sensor_owner_keys = jax.random.split(jax.random.fold_in(own_keys[8], 1), NSENS // SENS_DEV)
    sensor_owner_turns = jax.random.permutation(jax.random.fold_in(own_keys[8], 3), NSENS // SENS_DEV)
    sensor_owner = jax.vmap(lambda own, number: deal_out(jax.random.fold_in(own_keys[8], 2), own, number, SENS_DEV, N_LEAF, 1, CAP, 2))(sensor_owner_keys, sensor_owner_turns).reshape((NSENS, 1))
    sensor_row = place_ends(jax.random.randint(own_keys[9], (NSENS,), 0, LS // 2), jax.random.fold_in(own_keys[9], 1), 0, (LS // 2) - 1).astype(jnp.int32)
    sensor_weight = jnp.clip(jnp.exp(math.log(10.0) - 4.6051702 * jax.random.uniform(own_keys[10], (NSENS,), jnp.float32) ** shard_levels(own_keys[10], (NSENS,), ((0, 8),), -0.2, 0.2)), 0.1, 10.0)
    return {"leaf_inverse": leaf_inverse, "leaf_coupling": leaf_coupling, "leaf_rows": leaf_rows, "leaf_size": leaf_size, "sep_inverse": sep_inverse, "sep_coupling": sep_coupling, "rhs_leaf": rhs_leaf, "rhs_sep": rhs_sep, "sensor_owner": sensor_owner, "sensor_row": sensor_row, "sensor_weight": sensor_weight}


def height_of(index):
    value = index + 1
    height = 1
    while value % 2 == 0:
        value = value // 2
        height = height + 1
    return height


def ancestor(index, height):
    return ((index >> height) << height) + 2 ** (height - 1) - 1


def reference(leaf_inverse, leaf_coupling, leaf_rows, leaf_size, sep_inverse, sep_coupling, rhs_leaf, rhs_sep, sensor_owner, sensor_row, sensor_weight):
    leaf_rhs = rhs_leaf.reshape(N_LEAF, LS, NCOL)
    sep_rhs = rhs_sep.reshape(N_LEAF, SS, NCOL)
    live = (jnp.arange(LS)[None, :] < leaf_size[:, None]).astype(jnp.float32)[:, :, None]
    y_leaf = []
    contrib = []
    for leaf_index in range(N_LEAF):
        masked = (leaf_rhs[leaf_index] * live[leaf_index]).astype(jnp.bfloat16)
        solved = live[leaf_index] * jnp.dot(leaf_inverse[leaf_index], masked, preferred_element_type=jnp.float32)
        solved = solved.astype(jnp.bfloat16)
        y_leaf.append(solved)
        per_level = []
        for height in range(1, LEVELS + 1):
            product = jnp.dot(leaf_coupling[leaf_index, height - 1], solved, preferred_element_type=jnp.float32)
            placed = jnp.zeros((SS, NCOL), jnp.float32).at[leaf_rows[leaf_index, height - 1]].set(product)
            per_level.append(placed)
        contrib.append(per_level)
    y_sep = {}
    for height in range(1, LEVELS + 1):
        for owner_index in range(N_LEAF - 1):
            if height_of(owner_index) != height:
                continue
            first = (owner_index >> height) << height
            total = jnp.zeros((SS, NCOL), jnp.float32)
            for member in range(first, first + 2 ** height):
                total = total + contrib[member][height - 1]
                if member < N_LEAF - 1 and height_of(member) < height:
                    total = total + jnp.dot(sep_coupling[member, height - height_of(member) - 1], y_sep[member], preferred_element_type=jnp.float32)
            g_sep = (sep_rhs[owner_index].astype(jnp.float32) - total).astype(jnp.bfloat16)
            y_sep[owner_index] = jnp.dot(sep_inverse[owner_index], g_sep, preferred_element_type=jnp.float32).astype(jnp.bfloat16)
    x_sep = {}
    for height in range(LEVELS, 0, -1):
        for owner_index in range(N_LEAF - 1):
            if height_of(owner_index) != height:
                continue
            correction = jnp.zeros((SS, NCOL), jnp.float32)
            for upper in range(height + 1, LEVELS + 1):
                above = ancestor(owner_index, upper)
                correction = correction + jnp.dot(sep_coupling[owner_index, upper - height - 1].T, x_sep[above], preferred_element_type=jnp.float32)
            h_sep = (y_sep[owner_index].astype(jnp.float32) - correction).astype(jnp.bfloat16)
            x_sep[owner_index] = jnp.dot(sep_inverse[owner_index].T, h_sep, preferred_element_type=jnp.float32).astype(jnp.bfloat16)
    x_sep[N_LEAF - 1] = jnp.zeros((SS, NCOL), jnp.bfloat16)
    x_leaf = []
    for leaf_index in range(N_LEAF):
        correction = jnp.zeros((LS, NCOL), jnp.float32)
        for height in range(1, LEVELS + 1):
            above = x_sep[ancestor(leaf_index, height)]
            picked = above[leaf_rows[leaf_index, height - 1]]
            correction = correction + jnp.dot(leaf_coupling[leaf_index, height - 1].T, picked, preferred_element_type=jnp.float32)
        h_leaf = (y_leaf[leaf_index].astype(jnp.float32) - correction).astype(jnp.bfloat16)
        result = live[leaf_index] * jnp.dot(leaf_inverse[leaf_index].T, h_leaf, preferred_element_type=jnp.float32)
        x_leaf.append(result.astype(jnp.bfloat16))
    x_leaf_all = jnp.concatenate(x_leaf, axis=0)
    x_sep_all = jnp.concatenate([x_sep[owner_index] for owner_index in range(N_LEAF)], axis=0)
    position = (sensor_owner[:, 0] * LS + sensor_row).astype(jnp.int32)
    jacobian = x_leaf_all[position]
    weighted = (sensor_weight[:, None] * jacobian.astype(jnp.float32)).astype(jnp.bfloat16)
    gram = jnp.dot(jacobian.T, weighted, preferred_element_type=jnp.float32) / NSENS
    return x_leaf_all, x_sep_all, gram
```

```python
import functools

import jax
import jax.numpy as jnp
from jax import lax
from jax.experimental import pallas as pl
from jax.experimental.pallas import tpu as pltpu
from jax.sharding import PartitionSpec as P

F32, BF16 = jnp.float32, jnp.bfloat16
NN = (((1,), (0,)), ((), ()))
NT = (((1,), (1,)), ((), ()))
TN = (((0,), (0,)), ((), ()))
CHUNK = 256
LANES = 128


def mm(a, b, dims=NN):
    return lax.dot_general(a, b, dims, preferred_element_type=F32)


def remote(src, dst, send_sem, recv_sem, **place):
    return pltpu.make_async_remote_copy(
        src_ref=src,
        dst_ref=dst,
        send_sem=send_sem,
        recv_sem=recv_sem,
        device_id=place,
        device_id_type=pl.DeviceIdType.MESH,
    )


def kernel(
    n,
    reps,
    cols,
    total_sensors,
    a_hbm,
    coup_hbm,
    rows_ref,
    size_ref,
    s_hbm,
    u_hbm,
    b_hbm,
    rhs_hbm,
    owner_ref,
    srow_ref,
    weight_ref,
    xleaf_hbm,
    xsep_ref,
    gram_ref,
    a_v,
    b_v,
    coup_v,
    spread_v,
    y_v,
    h_v,
    x_v,
    xo_v,
    wx_v,
    s_anc,
    u_anc,
    r_anc,
    part_v,
    sbuf,
    rbuf,
    ysep,
    xfull,
    tab,
    tab_in,
    wpad,
    wcol,
    gs,
    gin,
    a_sem,
    in_sem,
    out_sem,
    anc_send,
    anc_recv,
    tab_send,
    tab_recv,
    bf_send,
    bf_recv,
    xs_send,
    xs_recv,
    col_send,
    col_recv,
    gr_send,
    gr_recv,
):
    depth = n.bit_length() - 1
    ls, nc = b_v.shape
    ss = s_anc.shape[1]
    hc = r_anc.shape[2]
    split = hc < nc
    sens_rows = xo_v.shape[1]
    nhi = sens_rows // LANES
    rb = gin.shape[1]
    per = hc // rb
    i = lax.axis_index("leaf")
    c = lax.axis_index("col")
    r = lax.axis_index("rep")
    half = pl.ds(pl.multiple_of(r * hc, hc), hc) if split else pl.ds(0, nc)
    nchunk = ls // CHUNK

    load_b = pltpu.make_async_copy(b_hbm, b_v, in_sem.at[0])
    load_b.start()
    load_c = pltpu.make_async_copy(coup_hbm.at[0], coup_v, in_sem.at[1])
    load_c.start()
    loads = [
        pltpu.make_async_copy(
            a_hbm.at[0, pl.ds(k * CHUNK, CHUNK)], a_v.at[pl.ds(k * CHUNK, CHUNK)], a_sem.at[k]
        )
        for k in range(nchunk)
    ]
    for load in loads:
        load.start()

    barrier = pltpu.get_barrier_semaphore()

    def greet(**place):
        pl.semaphore_signal(barrier, inc=1, device_id=place, device_id_type=pl.DeviceIdType.MESH)

    for j in range(n):
        for q in range(reps):
            @pl.when(jnp.logical_not((i == j) & (r == q)))
            def _():
                greet(leaf=j, rep=q)
    for step in range(1, cols):
        greet(col=lax.rem(c + step, cols))
    pl.semaphore_wait(barrier, n * reps + cols - 2)

    def anc_copies(level, slot):
        base = i // 2**level * 2**level
        dest = base + slot
        copies = [
            (s_hbm.at[0], s_anc.at[level - 1], 0),
            (rhs_hbm.at[:, half], r_anc.at[level - 1], 1),
        ]
        if level < depth:
            copies.append((u_hbm.at[0], u_anc.at[level - 1], 2))
        return dest, copies

    def owner_of(level):
        return i // 2**level * 2**level + 2 ** (level - 1) - 1

    for level in range(1, depth + 1):
        for slot in range(2**level):
            dest, copies = anc_copies(level, slot)

            @pl.when((i == owner_of(level)) & (dest == i))
            def _():
                for src, dst, kind in copies:
                    pltpu.make_async_copy(src, dst, anc_recv.at[level - 1, kind]).start()

            @pl.when((i == owner_of(level)) & (dest != i))
            def _():
                for src, dst, kind in copies:
                    remote(
                        src, dst, anc_send.at[slot, kind], anc_recv.at[level - 1, kind], leaf=dest
                    ).start()

    hi_key = owner_ref[...] * nhi + srow_ref[...] // LANES
    lo_key = srow_ref[...] % LANES
    sensors = hi_key.shape[1]
    hi_hot = (lax.broadcasted_iota(jnp.int32, (n * nhi, sensors), 0) == hi_key).astype(F32)
    hi_hot = hi_hot.astype(BF16)
    lo_hot = lax.broadcasted_iota(jnp.int32, (LANES, sensors), 0) == lo_key
    rest = weight_ref[...]
    table = jnp.zeros((n * nhi, LANES), F32)
    for _ in range(3):
        piece = rest.astype(BF16).astype(F32)
        table = table + mm(hi_hot, jnp.where(lo_hot, piece, 0.0).astype(BF16), NT)
        rest = rest - piece
    tab[...] = table
    here = i * reps + r
    for j in range(n):
        for q in range(reps):
            own = (i == j) & (r == q)

            @pl.when(own)
            def _():
                tab_in[here] = tab[pl.ds(j * nhi, nhi), :]

            @pl.when(jnp.logical_not(own))
            def _():
                remote(
                    tab.at[pl.ds(j * nhi, nhi)],
                    tab_in.at[here],
                    tab_send.at[j * reps + q],
                    tab_recv.at[here],
                    leaf=j,
                    rep=q,
                ).start()

    size = size_ref[0]

    def live(k):
        return lax.broadcasted_iota(jnp.int32, (CHUNK, nc), 0) + k * CHUNK < size

    load_b.wait()
    for k in range(nchunk):
        rows = pl.ds(k * CHUNK, CHUNK)
        b_v[rows, :] = jnp.where(live(k), b_v[rows, :].astype(F32), 0.0).astype(BF16)
    load_c.wait()
    for level in range(depth):
        hot = lax.broadcasted_iota(jnp.int32, (ss, rows_ref.shape[2]), 0) == rows_ref[
            0, pl.ds(level, 1), :
        ]
        spread_v[pl.ds(level * ss, ss), :] = mm(
            hot.astype(F32).astype(BF16), coup_v[level]
        ).astype(BF16)
    for k in range(nchunk):
        rows = pl.ds(k * CHUNK, CHUNK)
        loads[k].wait()
        y_v[rows, :] = jnp.where(live(k), mm(a_v[rows, :], b_v[...]), 0.0).astype(BF16)
        product = mm(spread_v[:, rows], y_v[rows, half])
        part_v[...] = product if k == 0 else part_v[...] + product

    def wait_anc(level, kind):
        _, copies = anc_copies(level, 0)
        src, dst, which = copies[kind]
        pltpu.make_async_copy(src, dst, anc_recv.at[level - 1, which]).wait()

    sent = []
    for level in range(1, depth + 1):
        partner = i ^ (1 << (level - 1))
        stage = level - 1
        pieces = [(pl.ds(level - 1, 1), 0)]
        if level < depth:
            pieces.append((pl.ds(level, depth - level), 1))
        copies = []
        for span, which in pieces:
            for m in range(span.start, span.start + span.size):
                sbuf[stage, m] = part_v[pl.ds(m * ss, ss), :].astype(BF16)
            copy = remote(
                sbuf.at[stage, span],
                rbuf.at[stage, span],
                bf_send.at[stage, which],
                bf_recv.at[stage, which],
                leaf=partner,
            )
            copy.start()
            copies.append(copy)
        sent += copies
        if level == 1:
            for j in range(n):
                for q in range(reps):
                    @pl.when(jnp.logical_not((i == j) & (r == q)))
                    def _():
                        remote(
                            tab.at[pl.ds(0, nhi)],
                            tab_in.at[j * reps + q],
                            tab_send.at[0],
                            tab_recv.at[j * reps + q],
                            rep=1 - r,
                        ).wait_recv()
            wpad[...] = jnp.zeros_like(wpad)
            weights = tab_in[0]
            for j in range(1, n * reps):
                weights = weights + tab_in[j]
            wpad[pl.ds(0, nhi), :] = weights
            wcol[...] = wpad[...].T
        wait_anc(level, 0)
        wait_anc(level, 1)
        if level < depth:
            wait_anc(level, 2)
        copies[0].wait_recv()
        total = part_v[pl.ds(stage * ss, ss), :] + rbuf[stage, stage].astype(F32)
        g = (r_anc[stage].astype(F32) - total).astype(BF16)
        y_here = mm(s_anc[stage], g).astype(BF16)
        ysep[stage] = y_here
        if level < depth:
            copies[1].wait_recv()
            for m in range(level, depth):
                span = pl.ds(m * ss, ss)
                part_v[span, :] = (
                    part_v[span, :]
                    + rbuf[stage, m].astype(F32)
                    + mm(u_anc[stage, m - level], y_here)
                )

    solved = {}
    shared = []
    for level in range(depth, 0, -1):
        stage = level - 1
        h_here = ysep[stage]
        if level < depth:
            correction = mm(u_anc[stage, 0], solved[level + 1], TN)
            for upper in range(level + 2, depth + 1):
                correction = correction + mm(u_anc[stage, upper - level - 1], solved[upper], TN)
            h_here = (h_here.astype(F32) - correction).astype(BF16)
        solved[level] = mm(s_anc[stage], h_here, TN).astype(BF16)
        span = pl.ds(stage * ss, ss)
        xfull[span, half] = solved[level]
        if split:
            copy = remote(
                xfull.at[span, half], xfull.at[span, half], xs_send.at[stage], xs_recv.at[stage],
                rep=1 - r,
            )
            copy.start()
            shared.append(copy)
    sent += shared
    for copy in shared:
        copy.wait_recv()
    for k in range(nchunk):
        rows = pl.ds(k * CHUNK, CHUNK)
        h_v[rows, :] = (
            y_v[rows, :].astype(F32) - mm(spread_v[:, rows], xfull[...], TN)
        ).astype(BF16)

    outs = []
    from_col = {}

    def back_solve(k):
        rows = pl.ds(k * CHUNK, CHUNK)
        x_v[rows, :] = jnp.where(live(k), mm(a_v[:, rows], h_v[...], TN), 0.0).astype(BF16)
        if k * CHUNK < sens_rows:
            for step in range(1, cols):
                copy = remote(
                    x_v.at[rows, half],
                    xo_v.at[step - 1, rows],
                    col_send.at[step - 1, k],
                    col_recv.at[step - 1, k],
                    col=lax.rem(c + step, cols),
                )
                copy.start()
                from_col[step, k] = copy
        out = pltpu.make_async_copy(x_v.at[rows], xleaf_hbm.at[rows], out_sem.at[k])
        out.start()
        outs.append(out)

    nsens = sens_rows // CHUNK
    for k in range(nsens):
        back_solve(k)
    sent += list(from_col.values())
    for k in range(nhi):
        rows = pl.ds(k * LANES, LANES)
        wx_v[rows, :] = (x_v[rows, :].astype(F32) * wcol[:, k : k + 1]).astype(BF16)

    def scatter_gram(b, wait):
        block = lax.rem(c + cols - b, cols)
        group = block * reps + r if split else block
        for t in range(per):
            dest = group * per + t
            if not split and t % reps == 0:
                dest = dest + r
            elif not split:
                continue
            own = (dest // reps == i) & (dest % reps == r)
            span = pl.ds(t * rb, rb) if split else pl.ds(pl.multiple_of((t + r) * rb, rb), rb)

            if not wait:
                @pl.when(own)
                def _():
                    gin[i] = gs[b, span, :]

            @pl.when(jnp.logical_not(own))
            def _():
                copy = remote(
                    gs.at[b, span],
                    gin.at[i],
                    gr_send.at[b, t],
                    gr_recv.at[i],
                    leaf=dest // reps,
                    rep=dest % reps,
                )
                if wait:
                    copy.wait_send()
                else:
                    copy.start()

    gs[0] = mm(x_v[pl.ds(0, sens_rows), half], wx_v[...], TN).astype(gs.dtype)
    scatter_gram(0, False)
    for k in range(nsens, nchunk):
        back_solve(k)
    for b in range(1, cols):
        other = jnp.zeros((hc, nc), F32)
        for k in range(nsens):
            rows = pl.ds(k * CHUNK, CHUNK)
            from_col[b, k].wait_recv()
            other = other + mm(xo_v[b - 1, rows, :], wx_v[rows, :], TN)
        gs[b] = other.astype(gs.dtype)
        scatter_gram(b, False)

    xsep_ref[...] = jnp.zeros_like(xsep_ref)
    for level in range(1, depth + 1):
        @pl.when(i == owner_of(level))
        def _():
            xsep_ref[...] = xfull[pl.ds((level - 1) * ss, ss), :]

    for copy in sent:
        copy.wait_send()
    for level in range(1, depth + 1):
        for slot in range(2**level):
            dest, copies = anc_copies(level, slot)

            @pl.when((i == owner_of(level)) & (dest != i))
            def _():
                for src, dst, kind in copies:
                    remote(
                        src, dst, anc_send.at[slot, kind], anc_recv.at[level - 1, kind], leaf=dest
                    ).wait_send()
    for j in range(n):
        for q in range(reps):
            @pl.when(jnp.logical_not((i == j) & (r == q)))
            def _():
                remote(
                    tab.at[pl.ds(j * nhi, nhi)],
                    tab_in.at[here],
                    tab_send.at[j * reps + q],
                    tab_recv.at[here],
                    leaf=j,
                    rep=q,
                ).wait_send()
    for out in outs:
        out.wait()

    sender = here // per % reps if split else r
    for j in range(n):
        @pl.when(jnp.logical_not((i == j) & (sender == r)))
        def _():
            remote(
                gs.at[0, pl.ds(0, rb)], gin.at[j], gr_send.at[0, 0], gr_recv.at[j], rep=1 - r
            ).wait_recv()
    gram = gin[0].astype(F32)
    for j in range(1, n):
        gram = gram + gin[j].astype(F32)
    gram_ref[...] = gram / total_sensors
    for b in range(cols):
        scatter_gram(b, True)


def body(
    leaf_inverse,
    leaf_coupling,
    leaf_rows,
    leaf_size,
    sep_inverse,
    sep_coupling,
    rhs_leaf,
    rhs_sep,
    sensor_owner,
    sensor_row,
    sensor_weight,
):
    n = lax.axis_size("leaf")
    reps = lax.axis_size("rep")
    cols = lax.axis_size("col")
    depth = n.bit_length() - 1
    ls, nc = rhs_leaf.shape
    ss = sep_inverse.shape[1]
    kr = leaf_coupling.shape[2]
    slots = sep_coupling.shape[1]
    hc = nc // reps if nc // reps % LANES == 0 else nc
    sens = sensor_row.shape[0]
    sens_rows = ls // 2
    nhi = sens_rows // LANES
    rb = nc * cols // (n * reps)
    gram_type = BF16 if rb % 16 == 0 else F32
    nchunk = ls // CHUNK
    dma = pltpu.SemaphoreType.DMA
    hbm = pl.BlockSpec(memory_space=pl.ANY)
    vmem = pl.BlockSpec(memory_space=pltpu.VMEM)
    smem = pl.BlockSpec(memory_space=pltpu.SMEM)
    return pl.pallas_call(
        functools.partial(kernel, n, reps, cols, sens * n * reps),
        out_shape=(
            jax.ShapeDtypeStruct((ls, nc), BF16),
            jax.ShapeDtypeStruct((ss, nc), BF16),
            jax.ShapeDtypeStruct((rb, nc), F32),
        ),
        in_specs=[hbm, hbm, vmem, smem, hbm, hbm, hbm, hbm, vmem, vmem, vmem],
        out_specs=(hbm, vmem, vmem),
        scratch_shapes=[
            pltpu.VMEM((ls, ls), BF16),
            pltpu.VMEM((ls, nc), BF16),
            pltpu.VMEM((depth, kr, ls), BF16),
            pltpu.VMEM((depth * ss, ls), BF16),
            pltpu.VMEM((ls, nc), BF16),
            pltpu.VMEM((ls, nc), BF16),
            pltpu.VMEM((ls, nc), BF16),
            pltpu.VMEM((cols - 1, sens_rows, hc), BF16),
            pltpu.VMEM((sens_rows, nc), BF16),
            pltpu.VMEM((depth, ss, ss), BF16),
            pltpu.VMEM((depth, slots, ss, ss), BF16),
            pltpu.VMEM((depth, ss, hc), BF16),
            pltpu.VMEM((depth * ss, hc), F32),
            pltpu.VMEM((depth, depth, ss, hc), BF16),
            pltpu.VMEM((depth, depth, ss, hc), BF16),
            pltpu.VMEM((depth, ss, hc), BF16),
            pltpu.VMEM((depth * ss, nc), BF16),
            pltpu.VMEM((n * nhi, LANES), F32),
            pltpu.VMEM((n * reps, nhi, LANES), F32),
            pltpu.VMEM((LANES, LANES), F32),
            pltpu.VMEM((LANES, LANES), F32),
            pltpu.VMEM((cols, hc, nc), gram_type),
            pltpu.VMEM((n, rb, nc), gram_type),
            dma((nchunk,)),
            dma((2,)),
            dma((nchunk,)),
            dma((n, 3)),
            dma((depth, 3)),
            dma((n * reps,)),
            dma((n * reps,)),
            dma((depth, 2)),
            dma((depth, 2)),
            dma((depth,)),
            dma((depth,)),
            dma((cols - 1, nchunk)),
            dma((cols - 1, nchunk)),
            dma((cols, hc // rb)),
            dma((n,)),
        ],
        compiler_params=pltpu.CompilerParams(
            collective_id=0, has_side_effects=True, vmem_limit_bytes=52 * 2**20
        ),
        name="solve_and_gram",
    )(
        leaf_inverse,
        leaf_coupling,
        leaf_rows,
        leaf_size,
        sep_inverse,
        sep_coupling,
        rhs_leaf,
        rhs_sep,
        sensor_owner.reshape(1, sens),
        sensor_row.reshape(1, sens),
        sensor_weight.reshape(1, sens),
    )


def solution(mesh):
    placed = (
        P(("parts", "leaf"), None, None),
        P(("parts", "leaf"), None, None, None),
        P(("parts", "leaf"), None, None),
        P(("parts", "leaf")),
        P(("parts", "leaf"), None, None),
        P(("parts", "leaf"), None, None, None),
        P(("parts", "leaf"), "col"),
        P(("parts", "leaf"), "col"),
        P(("parts", "leaf", "rep"), None),
        P(("parts", "leaf", "rep")),
        P(("parts", "leaf", "rep")),
    )
    return jax.shard_map(
        body,
        mesh=mesh,
        in_specs=placed,
        out_specs=(
            P(("parts", "leaf"), "col"),
            P(("parts", "leaf"), "col"),
            P(("parts", "leaf", "rep"), "col"),
        ),
        check_vma=False,
    )
```

```python
import functools

import jax
import jax.numpy as jnp
from jax import lax
from jax.experimental import pallas as pl
from jax.experimental.pallas import tpu as pltpu
from jax.sharding import PartitionSpec as P

F32, BF16 = jnp.float32, jnp.bfloat16
NN = (((1,), (0,)), ((), ()))
NT = (((1,), (1,)), ((), ()))
TN = (((0,), (0,)), ((), ()))
CHUNK = 256
LANES = 128


def mm(a, b, dims=NN):
    return lax.dot_general(a, b, dims, preferred_element_type=F32)


def remote(src, dst, send_sem, recv_sem, **place):
    return pltpu.make_async_remote_copy(
        src_ref=src,
        dst_ref=dst,
        send_sem=send_sem,
        recv_sem=recv_sem,
        device_id=place,
        device_id_type=pl.DeviceIdType.MESH,
    )


def kernel(
    n,
    reps,
    cols,
    total_sensors,
    a_hbm,
    coup_hbm,
    rows_hbm,
    size_ref,
    s_hbm,
    u_hbm,
    b_hbm,
    rhs_hbm,
    owner_hbm,
    srow_hbm,
    weight_hbm,
    xleaf_hbm,
    xsep_ref,
    gram_ref,
    a_v,
    b_v,
    coup_v,
    spread_v,
    y_v,
    h_v,
    x_v,
    xo_v,
    wx_v,
    s_anc,
    u_anc,
    r_anc,
    part_v,
    sbuf,
    rbuf,
    ysep,
    xfull,
    tab,
    tab_in,
    wpad,
    wcol,
    rows_ref,
    rows_in,
    owner_ref,
    srow_ref,
    weight_ref,
    comp_v,
    cs,
    cr,
    gs,
    gin,
    a_sem,
    in_sem,
    out_sem,
    anc_send,
    anc_recv,
    fwd_send,
    tab_send,
    tab_recv,
    bf_send,
    bf_recv,
    xs_send,
    xs_recv,
    col_send,
    col_recv,
    gr_send,
    gr_recv,
):
    depth = n.bit_length() - 1
    ls, nc = b_v.shape
    ss = s_anc.shape[1]
    hc = r_anc.shape[2]
    split = hc < nc
    sens_rows = xo_v.shape[1]
    nhi = sens_rows // LANES
    rb = gin.shape[1]
    per = hc // rb
    i = lax.axis_index("leaf")
    c = lax.axis_index("col")
    r = lax.axis_index("rep")
    half = pl.ds(pl.multiple_of(r * hc, hc), hc) if split else pl.ds(0, nc)
    nchunk = ls // CHUNK

    barrier = pltpu.get_barrier_semaphore()

    def greet(**place):
        pl.semaphore_signal(barrier, inc=1, device_id=place, device_id_type=pl.DeviceIdType.MESH)

    for j in range(n):
        for q in range(reps):
            @pl.when(jnp.logical_not((i == j) & (r == q)))
            def _():
                greet(leaf=j, rep=q)
    for step in range(1, cols):
        greet(col=lax.rem(c + step, cols))

    load_b = pltpu.make_async_copy(b_hbm, b_v, in_sem.at[0])
    load_b.start()
    smalls = [
        pltpu.make_async_copy(src, dst, in_sem.at[2 + k])
        for k, (src, dst) in enumerate(
            (
                (rows_hbm.at[0], rows_ref),
                (owner_hbm, owner_ref),
                (srow_hbm, srow_ref),
                (weight_hbm, weight_ref),
            )
        )
    ]
    for load in smalls:
        load.start()
    load_c = pltpu.make_async_copy(coup_hbm.at[0], coup_v, in_sem.at[1])
    load_c.start()
    loads = [
        pltpu.make_async_copy(
            a_hbm.at[0, pl.ds(k * CHUNK, CHUNK)], a_v.at[pl.ds(k * CHUNK, CHUNK)], a_sem.at[k]
        )
        for k in range(nchunk)
    ]
    for load in loads:
        load.start()
    pl.semaphore_wait(barrier, n * reps + cols - 2)

    hs = ss // reps
    mine = pl.ds(pl.multiple_of(r * hs, hs), hs)
    theirs = pl.ds(pl.multiple_of((1 - r) * hs, hs), hs)

    def anc_copies(level, local):
        copies = [
            (s_hbm.at[0, mine], s_anc.at[level - 1, mine], 0),
            (rhs_hbm.at[:, half], r_anc.at[level - 1], 1),
        ]
        if level < depth:
            copies.append((u_hbm.at[0, :, mine], u_anc.at[level - 1, :, mine], 2))
        if local:
            copies.append((s_hbm.at[0, theirs], s_anc.at[level - 1, theirs], 3))
            if level < depth:
                copies.append((u_hbm.at[0, :, theirs], u_anc.at[level - 1, :, theirs], 4))
        return copies

    def owner_of(level):
        return i // 2**level * 2**level + 2 ** (level - 1) - 1

    def each_dest(level, act):
        for slot in range(2**level):
            if slot == 2 ** (level - 1) - 1:
                continue

            @pl.when(i == owner_of(level))
            def _():
                for src, dst, kind in anc_copies(level, False):
                    act(
                        remote(
                            src,
                            dst,
                            anc_send.at[slot, kind],
                            anc_recv.at[level - 1, kind],
                            leaf=i // 2**level * 2**level + slot,
                        )
                    )

    for level in range(1, depth + 1):
        each_dest(level, lambda copy: copy.start())

        @pl.when(i == owner_of(level))
        def _():
            for src, dst, kind in anc_copies(level, True):
                pltpu.make_async_copy(src, dst, anc_recv.at[level - 1, kind]).start()

    def wait_anc(level, kinds):
        for src, dst, kind in anc_copies(level, True):
            if kind in kinds:
                pltpu.make_async_copy(src, dst, anc_recv.at[level - 1, kind]).wait()

    def relay_copies(level):
        blocks = [(s_anc.at[level - 1, mine], 3)]
        if level < depth:
            blocks.append((u_anc.at[level - 1, :, mine], 4))
        return [
            remote(
                block,
                block,
                fwd_send.at[level - 1, kind - 3],
                anc_recv.at[level - 1, kind],
                rep=1 - r,
            )
            for block, kind in blocks
        ]

    def relay(level):
        wait_anc(level, (0, 2))

        @pl.when(i != owner_of(level))
        def _():
            for copy in relay_copies(level):
                copy.start()

    for load in smalls:
        load.wait()
    row_copy = remote(rows_ref, rows_in, in_sem.at[6], in_sem.at[7], leaf=i ^ 1)
    row_copy.start()

    hi_key = owner_ref[...] * nhi + srow_ref[...] // LANES
    lo_key = srow_ref[...] % LANES
    sensors = hi_key.shape[1]
    hi_hot = (lax.broadcasted_iota(jnp.int32, (n * nhi, sensors), 0) == hi_key).astype(F32)
    hi_hot = hi_hot.astype(BF16)
    lo_hot = lax.broadcasted_iota(jnp.int32, (LANES, sensors), 0) == lo_key
    rest = weight_ref[...]
    table = jnp.zeros((n * nhi, LANES), F32)
    for _ in range(3):
        piece = rest.astype(BF16).astype(F32)
        table = table + mm(hi_hot, jnp.where(lo_hot, piece, 0.0).astype(BF16), NT)
        rest = rest - piece
    tab[...] = table
    here = i * reps + r
    for j in range(n):
        for q in range(reps):
            own = (i == j) & (r == q)

            @pl.when(own)
            def _():
                tab_in[here] = tab[pl.ds(j * nhi, nhi), :]

            @pl.when(jnp.logical_not(own))
            def _():
                remote(
                    tab.at[pl.ds(j * nhi, nhi)],
                    tab_in.at[here],
                    tab_send.at[j * reps + q],
                    tab_recv.at[here],
                    leaf=j,
                    rep=q,
                ).start()

    size = size_ref[0]

    def live(k):
        return lax.broadcasted_iota(jnp.int32, (CHUNK, nc), 0) + k * CHUNK < size

    load_b.wait()
    for k in range(nchunk):
        rows = pl.ds(k * CHUNK, CHUNK)
        b_v[rows, :] = jnp.where(live(k), b_v[rows, :].astype(F32), 0.0).astype(BF16)
    load_c.wait()
    for level in range(depth):
        hot = lax.broadcasted_iota(jnp.int32, (ss, rows_ref.shape[1]), 0) == rows_ref[
            pl.ds(level, 1), :
        ]
        spread_v[pl.ds(level * ss, ss), :] = mm(
            hot.astype(F32).astype(BF16), coup_v[level]
        ).astype(BF16)
    for k in range(nchunk):
        rows = pl.ds(k * CHUNK, CHUNK)
        loads[k].wait()
        y_v[rows, :] = jnp.where(live(k), mm(a_v[rows, :], b_v[...]), 0.0).astype(BF16)
        product = mm(spread_v[:, rows], y_v[rows, half])
        part_v[...] = product if k == 0 else part_v[...] + product
        for level in range(depth):
            product = mm(coup_v[level, :, rows], y_v[rows, half])
            comp_v[level] = product if k == 0 else comp_v[level] + product

    sent = [row_copy]
    for level in range(1, depth + 1):
        partner = i ^ (1 << (level - 1))
        stage = level - 1
        pieces = [(pl.ds(level - 1, 1), 0)]
        if level < depth:
            pieces.append((pl.ds(level, depth - level), 1))
        copies = []
        for span, which in pieces:
            for m in range(span.start, span.start + span.size):
                if stage == 0:
                    cs[m] = comp_v[m].astype(BF16)
                else:
                    sbuf[stage - 1, m] = part_v[pl.ds(m * ss, ss), :].astype(BF16)
            copy = remote(
                cs.at[span] if stage == 0 else sbuf.at[stage - 1, span],
                cr.at[span] if stage == 0 else rbuf.at[stage - 1, span],
                bf_send.at[stage, which],
                bf_recv.at[stage, which],
                leaf=partner,
            )
            copy.start()
            copies.append(copy)
        sent += copies
        if level == 1:
            for upper in range(1, depth + 1):
                relay(upper)
            row_copy.wait_recv()
            for j in range(n):
                for q in range(reps):
                    @pl.when(jnp.logical_not((i == j) & (r == q)))
                    def _():
                        remote(
                            tab.at[pl.ds(0, nhi)],
                            tab_in.at[j * reps + q],
                            tab_send.at[0],
                            tab_recv.at[j * reps + q],
                            rep=1 - r,
                        ).wait_recv()
            wpad[...] = jnp.zeros_like(wpad)
            weights = tab_in[0]
            for j in range(1, n * reps):
                weights = weights + tab_in[j]
            wpad[pl.ds(0, nhi), :] = weights
            wcol[...] = wpad[...].T

        def received(m):
            if level > 1:
                return rbuf[stage - 1, m].astype(F32)
            hot = lax.broadcasted_iota(jnp.int32, (ss, rows_in.shape[1]), 0) == rows_in[
                pl.ds(m, 1), :
            ]
            return mm(hot.astype(F32).astype(BF16), cr[m])

        wait_anc(level, (1, 3, 4))
        copies[0].wait_recv()
        total = part_v[pl.ds(stage * ss, ss), :] + received(stage)
        g = (r_anc[stage].astype(F32) - total).astype(BF16)
        y_here = mm(s_anc[stage], g).astype(BF16)
        ysep[stage] = y_here
        if level < depth:
            copies[1].wait_recv()
            for m in range(level, depth):
                span = pl.ds(m * ss, ss)
                part_v[span, :] = (
                    part_v[span, :]
                    + received(m)
                    + mm(u_anc[stage, m - level], y_here)
                )

    solved = {}
    shared = []
    for level in range(depth, 0, -1):
        stage = level - 1
        h_here = ysep[stage]
        if level < depth:
            correction = mm(u_anc[stage, 0], solved[level + 1], TN)
            for upper in range(level + 2, depth + 1):
                correction = correction + mm(u_anc[stage, upper - level - 1], solved[upper], TN)
            h_here = (h_here.astype(F32) - correction).astype(BF16)
        solved[level] = mm(s_anc[stage], h_here, TN).astype(BF16)
        span = pl.ds(stage * ss, ss)
        xfull[span, half] = solved[level]
        if split:
            copy = remote(
                xfull.at[span, half], xfull.at[span, half], xs_send.at[stage], xs_recv.at[stage],
                rep=1 - r,
            )
            copy.start()
            shared.append(copy)
    sent += shared
    for copy in shared:
        copy.wait_recv()
    for k in range(nchunk):
        rows = pl.ds(k * CHUNK, CHUNK)
        h_v[rows, :] = (
            y_v[rows, :].astype(F32) - mm(spread_v[:, rows], xfull[...], TN)
        ).astype(BF16)

    outs = []
    from_col = {}

    def back_solve(k):
        rows = pl.ds(k * CHUNK, CHUNK)
        x_v[rows, :] = jnp.where(live(k), mm(a_v[:, rows], h_v[...], TN), 0.0).astype(BF16)
        if k * CHUNK < sens_rows:
            for step in range(1, cols):
                copy = remote(
                    x_v.at[rows, half],
                    xo_v.at[step - 1, rows],
                    col_send.at[step - 1, k],
                    col_recv.at[step - 1, k],
                    col=lax.rem(c + step, cols),
                )
                copy.start()
                from_col[step, k] = copy
        out = pltpu.make_async_copy(x_v.at[rows], xleaf_hbm.at[rows], out_sem.at[k])
        out.start()
        outs.append(out)

    nsens = sens_rows // CHUNK
    for k in range(nsens):
        back_solve(k)
    sent += list(from_col.values())
    for k in range(nhi):
        rows = pl.ds(k * LANES, LANES)
        wx_v[rows, :] = (x_v[rows, :].astype(F32) * wcol[:, k : k + 1]).astype(BF16)

    def scatter_gram(b, wait):
        block = lax.rem(c + cols - b, cols)
        group = block * reps + r if split else block
        for t in range(per):
            dest = group * per + t
            if not split and t % reps == 0:
                dest = dest + r
            elif not split:
                continue
            own = (dest // reps == i) & (dest % reps == r)
            span = pl.ds(t * rb, rb) if split else pl.ds(pl.multiple_of((t + r) * rb, rb), rb)

            if not wait:
                @pl.when(own)
                def _():
                    gin[i] = gs[b, span, :]

            @pl.when(jnp.logical_not(own))
            def _():
                copy = remote(
                    gs.at[b, span],
                    gin.at[i],
                    gr_send.at[b, t],
                    gr_recv.at[i],
                    leaf=dest // reps,
                    rep=dest % reps,
                )
                if wait:
                    copy.wait_send()
                else:
                    copy.start()

    gs[0] = mm(x_v[pl.ds(0, sens_rows), half], wx_v[...], TN).astype(gs.dtype)
    scatter_gram(0, False)
    for k in range(nsens, nchunk):
        back_solve(k)
    for b in range(1, cols):
        other = jnp.zeros((hc, nc), F32)
        for k in range(nsens):
            rows = pl.ds(k * CHUNK, CHUNK)
            from_col[b, k].wait_recv()
            other = other + mm(xo_v[b - 1, rows, :], wx_v[rows, :], TN)
        gs[b] = other.astype(gs.dtype)
        scatter_gram(b, False)

    xsep_ref[...] = jnp.zeros_like(xsep_ref)
    for level in range(1, depth + 1):
        @pl.when(i == owner_of(level))
        def _():
            xsep_ref[...] = xfull[pl.ds((level - 1) * ss, ss), :]

    for copy in sent:
        copy.wait_send()
    for level in range(1, depth + 1):
        each_dest(level, lambda copy: copy.wait_send())

        @pl.when(i != owner_of(level))
        def _():
            for copy in relay_copies(level):
                copy.wait_send()

    for j in range(n):
        for q in range(reps):
            @pl.when(jnp.logical_not((i == j) & (r == q)))
            def _():
                remote(
                    tab.at[pl.ds(j * nhi, nhi)],
                    tab_in.at[here],
                    tab_send.at[j * reps + q],
                    tab_recv.at[here],
                    leaf=j,
                    rep=q,
                ).wait_send()
    for out in outs:
        out.wait()

    sender = here // per % reps if split else r
    for j in range(n):
        @pl.when(jnp.logical_not((i == j) & (sender == r)))
        def _():
            remote(
                gs.at[0, pl.ds(0, rb)], gin.at[j], gr_send.at[0, 0], gr_recv.at[j], rep=1 - r
            ).wait_recv()
    gram = gin[0].astype(F32)
    for j in range(1, n):
        gram = gram + gin[j].astype(F32)
    gram_ref[...] = gram / total_sensors
    for b in range(cols):
        scatter_gram(b, True)


def store(x_made, sep_made, gram_made, x_out, sep_out, gram_out, sem):
    copies = [
        pltpu.make_async_copy(src, dst, sem.at[k])
        for k, (src, dst) in enumerate(
            ((x_made, x_out), (sep_made, sep_out), (gram_made, gram_out))
        )
    ]
    for copy in copies:
        copy.start()
    for copy in copies:
        copy.wait()


def body(
    leaf_inverse,
    leaf_coupling,
    leaf_rows,
    leaf_size,
    sep_inverse,
    sep_coupling,
    rhs_leaf,
    rhs_sep,
    sensor_owner,
    sensor_row,
    sensor_weight,
):
    n = lax.axis_size("leaf")
    reps = lax.axis_size("rep")
    cols = lax.axis_size("col")
    depth = n.bit_length() - 1
    ls, nc = rhs_leaf.shape
    ss = sep_inverse.shape[1]
    kr = leaf_coupling.shape[2]
    slots = sep_coupling.shape[1]
    hc = nc // reps if nc // reps % LANES == 0 else nc
    sens = sensor_row.shape[0]
    sens_rows = ls // 2
    nhi = sens_rows // LANES
    rb = nc * cols // (n * reps)
    gram_type = BF16 if rb % 16 == 0 else F32
    nchunk = ls // CHUNK
    dma = pltpu.SemaphoreType.DMA
    anywhere = pl.BlockSpec(memory_space=pl.ANY)
    hbm = pl.BlockSpec(memory_space=pltpu.HBM)
    vmem = pl.BlockSpec(memory_space=pltpu.VMEM)
    smem = pl.BlockSpec(memory_space=pltpu.SMEM)
    made = pl.pallas_call(
        functools.partial(kernel, n, reps, cols, sens * n * reps),
        out_shape=(
            jax.ShapeDtypeStruct((ls, nc), BF16),
            jax.ShapeDtypeStruct((ss, nc), BF16),
            jax.ShapeDtypeStruct((rb, nc), F32),
        ),
        in_specs=[hbm, hbm, hbm, smem, hbm, hbm, hbm, hbm, hbm, hbm, hbm],
        out_specs=(anywhere, vmem, vmem),
        scratch_shapes=[
            pltpu.VMEM((ls, ls), BF16),
            pltpu.VMEM((ls, nc), BF16),
            pltpu.VMEM((depth, kr, ls), BF16),
            pltpu.VMEM((depth * ss, ls), BF16),
            pltpu.VMEM((ls, nc), BF16),
            pltpu.VMEM((ls, nc), BF16),
            pltpu.VMEM((ls, nc), BF16),
            pltpu.VMEM((cols - 1, sens_rows, hc), BF16),
            pltpu.VMEM((sens_rows, nc), BF16),
            pltpu.VMEM((depth, ss, ss), BF16),
            pltpu.VMEM((depth, slots, ss, ss), BF16),
            pltpu.VMEM((depth, ss, hc), BF16),
            pltpu.VMEM((depth * ss, hc), F32),
            pltpu.VMEM((max(depth - 1, 1), depth, ss, hc), BF16),
            pltpu.VMEM((max(depth - 1, 1), depth, ss, hc), BF16),
            pltpu.VMEM((depth, ss, hc), BF16),
            pltpu.VMEM((depth * ss, nc), BF16),
            pltpu.VMEM((n * nhi, LANES), F32),
            pltpu.VMEM((n * reps, nhi, LANES), F32),
            pltpu.VMEM((LANES, LANES), F32),
            pltpu.VMEM((LANES, LANES), F32),
            pltpu.VMEM((depth, kr), jnp.int32),
            pltpu.VMEM((depth, kr), jnp.int32),
            pltpu.VMEM((1, sens), jnp.int32),
            pltpu.VMEM((1, sens), jnp.int32),
            pltpu.VMEM((1, sens), F32),
            pltpu.VMEM((depth, kr, hc), F32),
            pltpu.VMEM((depth, kr, hc), BF16),
            pltpu.VMEM((depth, kr, hc), BF16),
            pltpu.VMEM((cols, hc, nc), gram_type),
            pltpu.VMEM((n, rb, nc), gram_type),
            dma((nchunk,)),
            dma((8,)),
            dma((nchunk,)),
            dma((n, 3)),
            dma((depth, 5)),
            dma((depth, 2)),
            dma((n * reps,)),
            dma((n * reps,)),
            dma((depth, 2)),
            dma((depth, 2)),
            dma((depth,)),
            dma((depth,)),
            dma((cols - 1, nchunk)),
            dma((cols - 1, nchunk)),
            dma((cols, hc // rb)),
            dma((n,)),
        ],
        compiler_params=pltpu.CompilerParams(
            collective_id=0, has_side_effects=True, vmem_limit_bytes=64 * 2**20 - 2**17
        ),
        name="solve_and_gram",
    )(
        leaf_inverse,
        leaf_coupling,
        leaf_rows,
        leaf_size,
        sep_inverse,
        sep_coupling,
        rhs_leaf,
        rhs_sep,
        sensor_owner.reshape(1, sens),
        sensor_row.reshape(1, sens),
        sensor_weight.reshape(1, sens),
    )
    return pl.pallas_call(
        store,
        out_shape=tuple(jax.ShapeDtypeStruct(part.shape, part.dtype) for part in made),
        in_specs=[anywhere] * 3,
        out_specs=(hbm,) * 3,
        scratch_shapes=[dma((3,))],
        name="store",
    )(*made)


def solution(mesh):
    placed = (
        P(("parts", "leaf"), None, None),
        P(("parts", "leaf"), None, None, None),
        P(("parts", "leaf"), None, None),
        P(("parts", "leaf")),
        P(("parts", "leaf"), None, None),
        P(("parts", "leaf"), None, None, None),
        P(("parts", "leaf"), "col"),
        P(("parts", "leaf"), "col"),
        P(("parts", "leaf", "rep"), None),
        P(("parts", "leaf", "rep")),
        P(("parts", "leaf", "rep")),
    )
    return jax.shard_map(
        body,
        mesh=mesh,
        in_specs=placed,
        out_specs=(
            P(("parts", "leaf"), "col"),
            P(("parts", "leaf"), "col"),
            P(("parts", "leaf", "rep"), "col"),
        ),
        check_vma=False,
    )
```

```python
import functools

import jax
import jax.numpy as jnp
from jax import lax
from jax.experimental import pallas as pl
from jax.experimental.pallas import tpu as pltpu
from jax.sharding import PartitionSpec as P

F32, BF16 = jnp.float32, jnp.bfloat16
NN = (((1,), (0,)), ((), ()))
NT = (((1,), (1,)), ((), ()))
TN = (((0,), (0,)), ((), ()))
CHUNK = 256
LANES = 128


def mm(a, b, dims=NN):
    return lax.dot_general(a, b, dims, preferred_element_type=F32)


def remote(src, dst, send_sem, recv_sem, **place):
    return pltpu.make_async_remote_copy(
        src_ref=src,
        dst_ref=dst,
        send_sem=send_sem,
        recv_sem=recv_sem,
        device_id=place,
        device_id_type=pl.DeviceIdType.MESH,
    )


def kernel(
    n,
    reps,
    cols,
    total_sensors,
    a_hbm,
    coup_hbm,
    rows_hbm,
    size_ref,
    s_hbm,
    u_hbm,
    b_hbm,
    rhs_hbm,
    owner_hbm,
    srow_hbm,
    weight_hbm,
    xleaf_hbm,
    xsep_ref,
    gram_ref,
    a_v,
    b_v,
    coup_v,
    spread_v,
    y_v,
    h_v,
    x_v,
    xo_v,
    wx_v,
    s_anc,
    u_anc,
    r_anc,
    part_v,
    sbuf,
    rbuf,
    ysep,
    xfull,
    tab,
    tab_in,
    wpad,
    wcol,
    rows_ref,
    rows_in,
    owner_ref,
    srow_ref,
    weight_ref,
    comp_v,
    cs,
    cr,
    gs,
    gin,
    a_sem,
    in_sem,
    out_sem,
    anc_send,
    anc_recv,
    fwd_send,
    tab_send,
    tab_recv,
    bf_send,
    bf_recv,
    xs_send,
    xs_recv,
    col_send,
    col_recv,
    gr_send,
    gr_recv,
):
    depth = n.bit_length() - 1
    ls, nc = b_v.shape
    ss = s_anc.shape[1]
    hc = r_anc.shape[2]
    split = hc < nc
    sens_rows = xo_v.shape[1]
    nhi = sens_rows // LANES
    rb = gin.shape[1]
    per = hc // rb
    i = lax.axis_index("leaf")
    c = lax.axis_index("col")
    r = lax.axis_index("rep")
    half = pl.ds(pl.multiple_of(r * hc, hc), hc) if split else pl.ds(0, nc)
    nchunk = ls // CHUNK

    barrier = pltpu.get_barrier_semaphore()

    def greet(**place):
        pl.semaphore_signal(barrier, inc=1, device_id=place, device_id_type=pl.DeviceIdType.MESH)

    for j in range(n):
        for q in range(reps):
            @pl.when(jnp.logical_not((i == j) & (r == q)))
            def _():
                greet(leaf=j, rep=q)
    for step in range(1, cols):
        greet(col=lax.rem(c + step, cols))

    load_b = pltpu.make_async_copy(b_hbm, b_v, in_sem.at[0])
    load_b.start()
    smalls = [
        pltpu.make_async_copy(src, dst, in_sem.at[2 + k])
        for k, (src, dst) in enumerate(
            (
                (rows_hbm.at[0], rows_ref),
                (owner_hbm, owner_ref),
                (srow_hbm, srow_ref),
                (weight_hbm, weight_ref),
            )
        )
    ]
    for load in smalls:
        load.start()
    load_c = pltpu.make_async_copy(coup_hbm.at[0], coup_v, in_sem.at[1])
    load_c.start()
    loads = [
        pltpu.make_async_copy(
            a_hbm.at[0, pl.ds(k * CHUNK, CHUNK)], a_v.at[pl.ds(k * CHUNK, CHUNK)], a_sem.at[k]
        )
        for k in range(nchunk)
    ]
    for load in loads:
        load.start()
    pl.semaphore_wait(barrier, n * reps + cols - 2)

    hs = ss // reps
    mine = pl.ds(pl.multiple_of(r * hs, hs), hs)
    theirs = pl.ds(pl.multiple_of((1 - r) * hs, hs), hs)

    def anc_copies(level, local):
        copies = [
            (s_hbm.at[0, mine], s_anc.at[level - 1, mine], 0),
            (rhs_hbm.at[:, half], r_anc.at[level - 1], 1),
        ]
        if level < depth:
            copies.append((u_hbm.at[0, :, mine], u_anc.at[level - 1, :, mine], 2))
        if local:
            copies.append((s_hbm.at[0, theirs], s_anc.at[level - 1, theirs], 3))
            if level < depth:
                copies.append((u_hbm.at[0, :, theirs], u_anc.at[level - 1, :, theirs], 4))
        return copies

    def owner_of(level):
        return i // 2**level * 2**level + 2 ** (level - 1) - 1

    def each_dest(level, act):
        for slot in range(2**level):
            if slot == 2 ** (level - 1) - 1:
                continue

            @pl.when(i == owner_of(level))
            def _():
                for src, dst, kind in anc_copies(level, False):
                    act(
                        remote(
                            src,
                            dst,
                            anc_send.at[slot, kind],
                            anc_recv.at[level - 1, kind],
                            leaf=i // 2**level * 2**level + slot,
                        )
                    )

    for level in range(1, depth + 1):
        each_dest(level, lambda copy: copy.start())

        @pl.when(i == owner_of(level))
        def _():
            for src, dst, kind in anc_copies(level, True):
                pltpu.make_async_copy(src, dst, anc_recv.at[level - 1, kind]).start()

    def wait_anc(level, kinds):
        for src, dst, kind in anc_copies(level, True):
            if kind in kinds:
                pltpu.make_async_copy(src, dst, anc_recv.at[level - 1, kind]).wait()

    def relay_copies(level):
        blocks = [(s_anc.at[level - 1, mine], 3)]
        if level < depth:
            blocks.append((u_anc.at[level - 1, :, mine], 4))
        return [
            remote(
                block,
                block,
                fwd_send.at[level - 1, kind - 3],
                anc_recv.at[level - 1, kind],
                rep=1 - r,
            )
            for block, kind in blocks
        ]

    def relay(level):
        wait_anc(level, (0, 2))

        @pl.when(i != owner_of(level))
        def _():
            for copy in relay_copies(level):
                copy.start()

    for load in smalls:
        load.wait()
    row_copy = remote(rows_ref, rows_in, in_sem.at[6], in_sem.at[7], leaf=i ^ 1)
    row_copy.start()

    hi_key = owner_ref[...] * nhi + srow_ref[...] // LANES
    lo_key = srow_ref[...] % LANES
    sensors = hi_key.shape[1]
    hi_hot = (lax.broadcasted_iota(jnp.int32, (n * nhi, sensors), 0) == hi_key).astype(F32)
    hi_hot = hi_hot.astype(BF16)
    lo_hot = lax.broadcasted_iota(jnp.int32, (LANES, sensors), 0) == lo_key
    rest = weight_ref[...]
    table = jnp.zeros((n * nhi, LANES), F32)
    for _ in range(3):
        piece = rest.astype(BF16).astype(F32)
        table = table + mm(hi_hot, jnp.where(lo_hot, piece, 0.0).astype(BF16), NT)
        rest = rest - piece
    tab[...] = table
    here = i * reps + r
    for j in range(n):
        for q in range(reps):
            own = (i == j) & (r == q)

            @pl.when(own)
            def _():
                tab_in[here] = tab[pl.ds(j * nhi, nhi), :]

            @pl.when(jnp.logical_not(own))
            def _():
                remote(
                    tab.at[pl.ds(j * nhi, nhi)],
                    tab_in.at[here],
                    tab_send.at[j * reps + q],
                    tab_recv.at[here],
                    leaf=j,
                    rep=q,
                ).start()

    size = size_ref[0]

    def live(k):
        return lax.broadcasted_iota(jnp.int32, (CHUNK, nc), 0) + k * CHUNK < size

    load_b.wait()
    for k in range(nchunk):
        rows = pl.ds(k * CHUNK, CHUNK)
        b_v[rows, :] = jnp.where(live(k), b_v[rows, :].astype(F32), 0.0).astype(BF16)
    load_c.wait()
    for level in range(depth):
        hot = lax.broadcasted_iota(jnp.int32, (ss, rows_ref.shape[1]), 0) == rows_ref[
            pl.ds(level, 1), :
        ]
        spread_v[pl.ds(level * ss, ss), :] = mm(
            hot.astype(F32).astype(BF16), coup_v[level]
        ).astype(BF16)
    for k in range(nchunk):
        rows = pl.ds(k * CHUNK, CHUNK)
        loads[k].wait()
        y_v[rows, :] = jnp.where(live(k), mm(a_v[rows, :], b_v[...]), 0.0).astype(BF16)
        product = mm(spread_v[:, rows], y_v[rows, half])
        part_v[...] = product if k == 0 else part_v[...] + product
        for level in range(depth):
            product = mm(coup_v[level, :, rows], y_v[rows, half])
            comp_v[level] = product if k == 0 else comp_v[level] + product

    sent = [row_copy]
    for level in range(1, depth + 1):
        partner = i ^ (1 << (level - 1))
        stage = level - 1
        pieces = [(pl.ds(level - 1, 1), 0)]
        if level < depth:
            pieces.append((pl.ds(level, depth - level), 1))
        copies = []
        for span, which in pieces:
            for m in range(span.start, span.start + span.size):
                if stage == 0:
                    cs[m] = comp_v[m].astype(BF16)
                else:
                    sbuf[stage - 1, m] = part_v[pl.ds(m * ss, ss), :].astype(BF16)
            copy = remote(
                cs.at[span] if stage == 0 else sbuf.at[stage - 1, span],
                cr.at[span] if stage == 0 else rbuf.at[stage - 1, span],
                bf_send.at[stage, which],
                bf_recv.at[stage, which],
                leaf=partner,
            )
            copy.start()
            copies.append(copy)
        sent += copies
        if level == 1:
            for upper in range(1, depth + 1):
                relay(upper)
            row_copy.wait_recv()
            for j in range(n):
                for q in range(reps):
                    @pl.when(jnp.logical_not((i == j) & (r == q)))
                    def _():
                        remote(
                            tab.at[pl.ds(0, nhi)],
                            tab_in.at[j * reps + q],
                            tab_send.at[0],
                            tab_recv.at[j * reps + q],
                            rep=1 - r,
                        ).wait_recv()
            wpad[...] = jnp.zeros_like(wpad)
            weights = tab_in[0]
            for j in range(1, n * reps):
                weights = weights + tab_in[j]
            wpad[pl.ds(0, nhi), :] = weights
            wcol[...] = wpad[...].T

        def received(m):
            if level > 1:
                return rbuf[stage - 1, m].astype(F32)
            hot = lax.broadcasted_iota(jnp.int32, (ss, rows_in.shape[1]), 0) == rows_in[
                pl.ds(m, 1), :
            ]
            return mm(hot.astype(F32).astype(BF16), cr[m])

        wait_anc(level, (1, 3, 4))
        copies[0].wait_recv()
        total = part_v[pl.ds(stage * ss, ss), :] + received(stage)
        g = (r_anc[stage].astype(F32) - total).astype(BF16)
        y_here = mm(s_anc[stage], g).astype(BF16)
        ysep[stage] = y_here
        if level < depth:
            copies[1].wait_recv()
            for m in range(level, depth):
                span = pl.ds(m * ss, ss)
                part_v[span, :] = (
                    part_v[span, :]
                    + received(m)
                    + mm(u_anc[stage, m - level], y_here)
                )

    solved = {}
    shared = []
    for level in range(depth, 0, -1):
        stage = level - 1
        h_here = ysep[stage]
        if level < depth:
            correction = mm(u_anc[stage, 0], solved[level + 1], TN)
            for upper in range(level + 2, depth + 1):
                correction = correction + mm(u_anc[stage, upper - level - 1], solved[upper], TN)
            h_here = (h_here.astype(F32) - correction).astype(BF16)
        solved[level] = mm(s_anc[stage], h_here, TN).astype(BF16)
        span = pl.ds(stage * ss, ss)
        xfull[span, half] = solved[level]
        if split:
            copy = remote(
                xfull.at[span, half], xfull.at[span, half], xs_send.at[stage], xs_recv.at[stage],
                rep=1 - r,
            )
            copy.start()
            shared.append(copy)
    sent += shared
    for copy in shared:
        copy.wait_recv()
    for k in range(nchunk):
        rows = pl.ds(k * CHUNK, CHUNK)
        h_v[rows, :] = (
            y_v[rows, :].astype(F32) - mm(spread_v[:, rows], xfull[...], TN)
        ).astype(BF16)

    outs = []
    from_col = {}

    def back_solve(k):
        rows = pl.ds(k * CHUNK, CHUNK)
        x_v[rows, :] = jnp.where(live(k), mm(a_v[:, rows], h_v[...], TN), 0.0).astype(BF16)
        if k * CHUNK < sens_rows:
            for step in range(1, cols):
                copy = remote(
                    x_v.at[rows, half],
                    xo_v.at[step - 1, rows],
                    col_send.at[step - 1, k],
                    col_recv.at[step - 1, k],
                    col=lax.rem(c + step, cols),
                )
                copy.start()
                from_col[step, k] = copy
        out = pltpu.make_async_copy(x_v.at[rows], xleaf_hbm.at[rows], out_sem.at[k])
        out.start()
        outs.append(out)

    nsens = sens_rows // CHUNK
    for k in range(nsens):
        back_solve(k)
    sent += list(from_col.values())
    for k in range(nhi):
        rows = pl.ds(k * LANES, LANES)
        wx_v[rows, :] = (x_v[rows, :].astype(F32) * wcol[:, k : k + 1]).astype(BF16)

    def scatter_gram(b, wait):
        block = lax.rem(c + cols - b, cols)
        group = block * reps + r if split else block
        for t in range(per):
            dest = group * per + t
            if not split and t % reps == 0:
                dest = dest + r
            elif not split:
                continue
            own = (dest // reps == i) & (dest % reps == r)
            span = pl.ds(t * rb, rb) if split else pl.ds(pl.multiple_of((t + r) * rb, rb), rb)

            if not wait:
                @pl.when(own)
                def _():
                    gin[i] = gs[b, span, :]

            @pl.when(jnp.logical_not(own))
            def _():
                copy = remote(
                    gs.at[b, span],
                    gin.at[i],
                    gr_send.at[b, t],
                    gr_recv.at[i],
                    leaf=dest // reps,
                    rep=dest % reps,
                )
                if wait:
                    copy.wait_send()
                else:
                    copy.start()

    gs[0] = mm(x_v[pl.ds(0, sens_rows), half], wx_v[...], TN).astype(gs.dtype)
    scatter_gram(0, False)
    for k in range(nsens, nchunk):
        back_solve(k)
    for b in range(1, cols):
        other = jnp.zeros((hc, nc), F32)
        for k in range(nsens):
            rows = pl.ds(k * CHUNK, CHUNK)
            from_col[b, k].wait_recv()
            other = other + mm(xo_v[b - 1, rows, :], wx_v[rows, :], TN)
        gs[b] = other.astype(gs.dtype)
        scatter_gram(b, False)

    xsep_ref[...] = jnp.zeros_like(xsep_ref)
    for level in range(1, depth + 1):
        @pl.when(i == owner_of(level))
        def _():
            xsep_ref[...] = xfull[pl.ds((level - 1) * ss, ss), :]

    for copy in sent:
        copy.wait_send()
    for level in range(1, depth + 1):
        each_dest(level, lambda copy: copy.wait_send())

        @pl.when(i != owner_of(level))
        def _():
            for copy in relay_copies(level):
                copy.wait_send()

    for j in range(n):
        for q in range(reps):
            @pl.when(jnp.logical_not((i == j) & (r == q)))
            def _():
                remote(
                    tab.at[pl.ds(j * nhi, nhi)],
                    tab_in.at[here],
                    tab_send.at[j * reps + q],
                    tab_recv.at[here],
                    leaf=j,
                    rep=q,
                ).wait_send()
    for out in outs:
        out.wait()

    sender = here // per % reps if split else r
    for j in range(n):
        @pl.when(jnp.logical_not((i == j) & (sender == r)))
        def _():
            remote(
                gs.at[0, pl.ds(0, rb)], gin.at[j], gr_send.at[0, 0], gr_recv.at[j], rep=1 - r
            ).wait_recv()
    gram = gin[0].astype(F32)
    for j in range(1, n):
        gram = gram + gin[j].astype(F32)
    gram_ref[...] = gram / total_sensors
    for b in range(cols):
        scatter_gram(b, True)


def store(pieces, *refs):
    made, outs, held, (load_sem, store_sem) = refs[:3], refs[3:6], refs[6:9], refs[9:]
    moves = []
    for k, (src, mid, dst) in enumerate(zip(made, held, outs)):
        size = src.shape[0] // pieces[k]
        for piece in range(pieces[k]):
            span = pl.ds(piece * size, size)
            sem = len(moves)
            moves.append(
                (
                    pltpu.make_async_copy(src.at[span], mid.at[span], load_sem.at[sem]),
                    pltpu.make_async_copy(mid.at[span], dst.at[span], store_sem.at[sem]),
                )
            )
    for load, _ in moves:
        load.start()
    for load, save in moves:
        load.wait()
        save.start()
    for _, save in moves:
        save.wait()


def body(
    leaf_inverse,
    leaf_coupling,
    leaf_rows,
    leaf_size,
    sep_inverse,
    sep_coupling,
    rhs_leaf,
    rhs_sep,
    sensor_owner,
    sensor_row,
    sensor_weight,
):
    n = lax.axis_size("leaf")
    reps = lax.axis_size("rep")
    cols = lax.axis_size("col")
    depth = n.bit_length() - 1
    ls, nc = rhs_leaf.shape
    ss = sep_inverse.shape[1]
    kr = leaf_coupling.shape[2]
    slots = sep_coupling.shape[1]
    hc = nc // reps if nc // reps % LANES == 0 else nc
    sens = sensor_row.shape[0]
    sens_rows = ls // 2
    nhi = sens_rows // LANES
    rb = nc * cols // (n * reps)
    gram_type = BF16 if rb % 16 == 0 else F32
    nchunk = ls // CHUNK
    dma = pltpu.SemaphoreType.DMA
    anywhere = pl.BlockSpec(memory_space=pl.ANY)
    hbm = pl.BlockSpec(memory_space=pltpu.HBM)
    vmem = pl.BlockSpec(memory_space=pltpu.VMEM)
    smem = pl.BlockSpec(memory_space=pltpu.SMEM)
    made = pl.pallas_call(
        functools.partial(kernel, n, reps, cols, sens * n * reps),
        out_shape=(
            jax.ShapeDtypeStruct((ls, nc), BF16),
            jax.ShapeDtypeStruct((ss, nc), BF16),
            jax.ShapeDtypeStruct((rb, nc), F32),
        ),
        in_specs=[hbm, hbm, hbm, smem, hbm, hbm, hbm, hbm, hbm, hbm, hbm],
        out_specs=(anywhere, vmem, vmem),
        scratch_shapes=[
            pltpu.VMEM((ls, ls), BF16),
            pltpu.VMEM((ls, nc), BF16),
            pltpu.VMEM((depth, kr, ls), BF16),
            pltpu.VMEM((depth * ss, ls), BF16),
            pltpu.VMEM((ls, nc), BF16),
            pltpu.VMEM((ls, nc), BF16),
            pltpu.VMEM((ls, nc), BF16),
            pltpu.VMEM((cols - 1, sens_rows, hc), BF16),
            pltpu.VMEM((sens_rows, nc), BF16),
            pltpu.VMEM((depth, ss, ss), BF16),
            pltpu.VMEM((depth, slots, ss, ss), BF16),
            pltpu.VMEM((depth, ss, hc), BF16),
            pltpu.VMEM((depth * ss, hc), F32),
            pltpu.VMEM((max(depth - 1, 1), depth, ss, hc), BF16),
            pltpu.VMEM((max(depth - 1, 1), depth, ss, hc), BF16),
            pltpu.VMEM((depth, ss, hc), BF16),
            pltpu.VMEM((depth * ss, nc), BF16),
            pltpu.VMEM((n * nhi, LANES), F32),
            pltpu.VMEM((n * reps, nhi, LANES), F32),
            pltpu.VMEM((LANES, LANES), F32),
            pltpu.VMEM((LANES, LANES), F32),
            pltpu.VMEM((depth, kr), jnp.int32),
            pltpu.VMEM((depth, kr), jnp.int32),
            pltpu.VMEM((1, sens), jnp.int32),
            pltpu.VMEM((1, sens), jnp.int32),
            pltpu.VMEM((1, sens), F32),
            pltpu.VMEM((depth, kr, hc), F32),
            pltpu.VMEM((depth, kr, hc), BF16),
            pltpu.VMEM((depth, kr, hc), BF16),
            pltpu.VMEM((cols, hc, nc), gram_type),
            pltpu.VMEM((n, rb, nc), gram_type),
            dma((nchunk,)),
            dma((8,)),
            dma((nchunk,)),
            dma((n, 3)),
            dma((depth, 5)),
            dma((depth, 2)),
            dma((n * reps,)),
            dma((n * reps,)),
            dma((depth, 2)),
            dma((depth, 2)),
            dma((depth,)),
            dma((depth,)),
            dma((cols - 1, nchunk)),
            dma((cols - 1, nchunk)),
            dma((cols, hc // rb)),
            dma((n,)),
        ],
        compiler_params=pltpu.CompilerParams(
            collective_id=0, has_side_effects=True, vmem_limit_bytes=64 * 2**20 - 2**17
        ),
        name="solve_and_gram",
    )(
        leaf_inverse,
        leaf_coupling,
        leaf_rows,
        leaf_size,
        sep_inverse,
        sep_coupling,
        rhs_leaf,
        rhs_sep,
        sensor_owner.reshape(1, sens),
        sensor_row.reshape(1, sens),
        sensor_weight.reshape(1, sens),
    )
    pieces = (nchunk, 1, 1)
    return pl.pallas_call(
        functools.partial(store, pieces),
        out_shape=tuple(jax.ShapeDtypeStruct(part.shape, part.dtype) for part in made),
        in_specs=[anywhere] * 3,
        out_specs=(anywhere,) * 3,
        scratch_shapes=[pltpu.VMEM(part.shape, part.dtype) for part in made]
        + [dma((sum(pieces),)), dma((sum(pieces),))],
        compiler_params=pltpu.CompilerParams(vmem_limit_bytes=64 * 2**20 - 2**17),
        name="store",
    )(*made)


def solution(mesh):
    placed = (
        P(("parts", "leaf"), None, None),
        P(("parts", "leaf"), None, None, None),
        P(("parts", "leaf"), None, None),
        P(("parts", "leaf")),
        P(("parts", "leaf"), None, None),
        P(("parts", "leaf"), None, None, None),
        P(("parts", "leaf"), "col"),
        P(("parts", "leaf"), "col"),
        P(("parts", "leaf", "rep"), None),
        P(("parts", "leaf", "rep")),
        P(("parts", "leaf", "rep")),
    )
    return jax.shard_map(
        body,
        mesh=mesh,
        in_specs=placed,
        out_specs=(
            P(("parts", "leaf"), "col"),
            P(("parts", "leaf"), "col"),
            P(("parts", "leaf", "rep"), "col"),
        ),
        check_vma=False,
    )
```
